256 devices in a mesh: tm: 16 (over x_hi, z), space: 16 (over x_lo, y, core).
Axes of the slice: x: 4 (x_hi: 2, x_lo: 2; x = x_hi * 2 + x_lo), y: 4, z: 8, core: 2. Of those that a mesh axis runs over, the one named last changes fastest.
Arguments:
- forcing: float32 [1024, 128, 2048], P('space', 'tm'), may hold values from -6 to 6
- kappa: float32 [1024, 2048], P('space'), may hold values from 0.12 to 0.24
- diag_coef: float32 [128], P('tm'), may hold values from 0.5 to 1.5
- lower_coef: float32 [128], P('tm'), may hold values from -0.6 to 0.6
- upper_coef: float32 [128], P('tm'), may hold values from -0.6 to 0.6
Outputs:
- result: float32 [1024, 128, 2048], P('space', 'tm')
The draws below stay inside these ranges and needn't reach their ends.
All inputs are finite; a program needn't handle non-finite values.
Results may differ from the reference program's by a relative error of at most 0.0003.
Values sent between devices are 32-bit elements; how exact they have to be, the bound alone decides.
No kernel may reach another device: no remote copies, remote signals or barrier semaphores. Data moves between devices by JAX's collectives and lax.ppermute only.
A program may use at most 128 MiB of HBM per device.

```python
import math
import jax
import jax.numpy as jnp
from jax import lax

NY = 2048
STEPS = 6
NX = 1024
SUBWIN = 128


def draw_kappa(key, part):
    key = jax.random.fold_in(key, 11)
    uniform_cells = jax.random.uniform(key, (NX, NY), jnp.float32)
    return (0.12 + 0.12 * uniform_cells).astype(jnp.float32)


def block_levels(own_key, dims, pieces, least, top_value):
    factor_of, own = 1.0, jax.random.fold_in(own_key, 6)
    for axis_at, shards_of in pieces:
        heights = jnp.exp(jax.random.uniform(jax.random.fold_in(own, axis_at), (shards_of,), jnp.float32, least / len(pieces), top_value / len(pieces)))
        factor_of = factor_of * jnp.repeat(heights, dims[axis_at] // shards_of).reshape([-1 if axis == axis_at else 1 for axis in range(len(dims))])
    return factor_of


def gaussian(own_key, dims, width, bound, cuts=(), kind=jnp.bfloat16):
    factor_of = block_levels(own_key, dims, cuts, -0.22, 0.18) if cuts else 1.0
    array = jax.random.normal(own_key, dims, jnp.float32) * width * factor_of
    return jnp.minimum(jnp.maximum(array, -bound), bound).astype(kind)


def setup_inputs(seed: int = 0) -> dict:
    arg_keys = jax.random.split(jax.random.key(seed), 6)
    return {
        "forcing": gaussian(arg_keys[0], (NX, SUBWIN, NY), 1.0, 6.0, ((0, 16), (1, 16)), jnp.float32),
        "kappa": draw_kappa(jax.random.fold_in(arg_keys[5], 71), 0),
        "diag_coef": jnp.clip(jnp.exp(math.log(1.5) - 1.0986123 * jax.random.uniform(arg_keys[2], (SUBWIN,), jnp.float32) ** block_levels(arg_keys[2], (SUBWIN,), ((0, 16),), -0.2, 0.2)), 0.5, 1.5),
        "lower_coef": jnp.clip(jax.random.uniform(arg_keys[3], (SUBWIN,), jnp.float32, -0.6, 0.6) * block_levels(arg_keys[3], (SUBWIN,), ((0, 16),), -0.4, 0.0), -0.6, 0.6),
        "upper_coef": jnp.clip(jax.random.uniform(arg_keys[4], (SUBWIN,), jnp.float32, -0.6, 0.6) * block_levels(arg_keys[4], (SUBWIN,), ((0, 16),), -0.4, 0.0), -0.6, 0.6),
    }


def single_diffusion_step(value_extended, kappa_extended):
    interface_rows = 0.5 * (kappa_extended[1:] + kappa_extended[:-1])
    flux_row_values = interface_rows * (value_extended[1:] - value_extended[:-1])
    div_rows = flux_row_values[1:] - flux_row_values[:-1]
    interior_slice = value_extended[1:-1]
    kin = kappa_extended[1:-1]
    zero_k = jnp.zeros_like(kin[:, :1])
    zero_v = jnp.zeros_like(interior_slice[:, :1])
    k_east = jnp.concatenate([kin[:, 1:], zero_k], axis=-1)
    k_west = jnp.concatenate([zero_k, kin[:, :-1]], axis=-1)
    value_eastward = jnp.concatenate([interior_slice[:, 1:], zero_v], axis=-1)
    v_west = jnp.concatenate([zero_v, interior_slice[:, :-1]], axis=-1)
    div_cols = 0.5 * (kin + k_east) * (value_eastward - interior_slice) - 0.5 * (k_west + kin) * (interior_slice - v_west)
    return interior_slice + div_rows + div_cols


def pad_rows(field):
    zero_row = jnp.zeros_like(field[:1])
    return jnp.concatenate([zero_row, field, zero_row], axis=0)


def reference(forcing, kappa, diag_coef, lower_coef, upper_coef):
    kappa_extended = pad_rows(kappa)
    count = forcing.shape[1]

    def one(index):
        later = jnp.minimum(index + 1, count - 1).astype(jnp.int32)
        earlier = jnp.maximum(index - 1, 0).astype(jnp.int32)
        has_later = (index + 1 < count).astype(jnp.float32)
        has_earlier = (index > 0).astype(jnp.float32)
        mixed = diag_coef[index] * forcing[:, index]
        mixed = mixed + has_later * lower_coef[later] * forcing[:, later]
        mixed = mixed + has_earlier * upper_coef[earlier] * forcing[:, earlier]
        for step in range(STEPS):
            mixed = single_diffusion_step(pad_rows(mixed), kappa_extended)
        return mixed

    stacked = lax.map(one, jnp.arange(count, dtype=jnp.int32))
    return jnp.moveaxis(stacked, 0, 1)
```

```python
import functools

import jax
import jax.numpy as jnp
from jax import lax
from jax.experimental import pallas as pl
from jax.experimental.pallas import tpu as pltpu
from jax.sharding import PartitionSpec as P

STEPS = 6
NV = 16
GV = NV + 2
LANES = 128
TILE = (8, LANES)
VMEM_LIMIT = 56 * 2**20
F32 = jnp.float32


def iota(dim):
    return lax.broadcasted_iota(jnp.int32, TILE, dim)


def to_columns(rows, scratch):
    scratch[...] = jnp.concatenate(rows, axis=0).T
    return [scratch[pl.ds(i, 8, stride=NV), :] for i in range(NV)]


def to_rows(columns, scratch):
    for i in range(NV):
        scratch[pl.ds(i, 8, stride=NV), :] = columns[i]
    flipped = scratch[...].T
    return [flipped[8 * j : 8 * j + 8] for j in range(NV)]


def ghost_west(last):
    turned = pltpu.roll(last, 1, 0)
    moved = jnp.where(iota(1) >= 8, pltpu.roll(turned, 8, 1), 0.0)
    return jnp.where(iota(0) == 0, moved, turned)


def ghost_east(first):
    turned = pltpu.roll(first, 7, 0)
    moved = jnp.where(iota(1) < LANES - 8, pltpu.roll(turned, LANES - 8, 1), 0.0)
    return jnp.where(iota(0) == 7, moved, turned)


def put_row(buffer, row, columns):
    for i in range(NV):
        buffer[row, i + 1] = columns[i]
    buffer[row, 0] = ghost_west(columns[NV - 1])
    buffer[row, NV + 1] = ghost_east(columns[0])


def mix_row(coef, row, field, before, after):
    slot = iota(0)
    mixed = []
    for j in range(NV):
        at = pl.ds(LANES * j, LANES)
        x = field[row, :, at]
        later = coef[1] * pltpu.roll(x, 7, 0)
        earlier = coef[2] * pltpu.roll(x, 1, 0)
        later = jnp.where(slot == 7, jnp.broadcast_to(after[row, :, at], TILE), later)
        earlier = jnp.where(slot == 0, jnp.broadcast_to(before[row, :, at], TILE), earlier)
        mixed.append(coef[0] * x + later + earlier)
    return mixed


def diffuse(src, dst, east, south, lo, count, shift=0, unroll=2, scale=None):
    def row_of(buffer, row):
        return [buffer[row, i + 1] for i in range(NV)]

    def finish(row, first, last):
        dst[row, 0] = ghost_west(last)
        dst[row, NV + 1] = ghost_east(first)

    def body(k, carry):
        row = lo + k
        v, north, (first, last) = carry[:NV], carry[NV : 2 * NV], carry[2 * NV :]
        finish(jnp.maximum(row - 1, lo), first, last)
        below = row_of(src, row + 1)
        west = east[row + shift, 0] * (v[0] - src[row, 0])
        new, flux = [], []
        for i in range(NV):
            v_east = v[i + 1] if i + 1 < NV else src[row, NV + 1]
            here = east[row + shift, i + 1] * (v_east - v[i])
            under = south[row + shift, i] * (below[i] - v[i])
            value = (v[i] + (here - west)) + (under - north[i])
            if scale is not None:
                value = value * scale(row)
            dst[row, i + 1] = value
            west = here
            flux.append(under)
            if i in (0, NV - 1):
                new.append(value)
        return (*below, *flux, *new)

    above, v = row_of(src, lo - 1), row_of(src, lo)
    north = [south[lo - 1 + shift, i] * (v[i] - above[i]) for i in range(NV)]
    out = lax.fori_loop(0, count, body, (*v, *north, v[0], v[NV - 1]), unroll=unroll)
    finish(lo + count - 1, *out[2 * NV :])


def coefficient_rows(half, east, south, lo, count, shift=0):
    def body(k, carry):
        row = lo + k
        here = [half[row, i] for i in range(GV)]
        for i in range(NV + 1):
            east[row + shift, i] = here[i] + here[i + 1]
        for i in range(NV):
            south[row + shift, i] = here[i + 1] + half[row + 1, i + 1]
        return carry

    lax.fori_loop(0, count, body, 0)


def faces_kernel(kappa, east, south, half, scratch):
    rows = kappa.shape[0]

    def block(b, carry):
        base = pl.multiple_of(b * 8, 8)
        part = kappa.at[pl.ds(base, 8), :]
        for q in range(8):
            spread = [jnp.broadcast_to(0.5 * part[q : q + 1, LANES * j : LANES * (j + 1)], TILE) for j in range(NV)]
            put_row(half, b * 8 + q, to_columns(spread, scratch.at[q]))
        return carry

    lax.fori_loop(0, rows // 8, block, 0)
    for i in range(GV):
        half[rows, i] = jnp.zeros(TILE, F32)
    coefficient_rows(half, east, south, 0, rows)


def faces(kappa):
    rows = kappa.shape[0]
    vmem = pl.BlockSpec(memory_space=pltpu.VMEM)
    return pl.pallas_call(
        faces_kernel,
        out_shape=(
            jax.ShapeDtypeStruct((rows, NV + 1, *TILE), F32),
            jax.ShapeDtypeStruct((rows, NV, *TILE), F32),
        ),
        in_specs=[vmem],
        out_specs=(vmem, vmem),
        scratch_shapes=[pltpu.VMEM((rows + 1, GV, *TILE), F32), pltpu.VMEM((8, LANES, LANES), F32)],
        compiler_params=pltpu.CompilerParams(vmem_limit_bytes=VMEM_LIMIT),
        cost_estimate=pl.CostEstimate(flops=10**7, bytes_accessed=9 * 2**20, transcendentals=0),
        name="faces",
    )(kappa)


def edges_kernel(coef, field_top, field_bottom, before, after, kappa_top, kappa_bottom, to_up, to_down):
    rows = before.shape[0]
    for side, field, kappa, start, out in ((0, field_top, kappa_top, 0, to_up), (1, field_bottom, kappa_bottom, rows - 8, to_down)):
        for k in range(STEPS):
            row = k if side == 0 else 2 + k
            mixed = mix_row(coef, row, field, before.at[pl.ds(start, 8)], after.at[pl.ds(start, 8)])
            for j in range(NV):
                out[k, :, pl.ds(LANES * j, LANES)] = mixed[j]
        out[STEPS] = kappa[...]


def edge_rows(coef, fields, before, after, kappa):
    rows, slots, width = fields.shape
    full = lambda shape: pl.BlockSpec(shape, lambda _: (0,) * len(shape))
    top, bottom = (lambda _: (0, 0, 0)), (lambda _: (rows // 8 - 1, 0, 0))
    out = jax.ShapeDtypeStruct((STEPS + 1, slots, width), F32)
    return pl.pallas_call(
        edges_kernel,
        grid=(1,),
        out_shape=(out, out),
        in_specs=[
            full(coef.shape),
            pl.BlockSpec((8, slots, width), top),
            pl.BlockSpec((8, slots, width), bottom),
            full(before.shape),
            full(after.shape),
            pl.BlockSpec((8, width), lambda _: (0, 0)),
            pl.BlockSpec((8, width), lambda _: (rows // 8 - 1, 0)),
        ],
        out_specs=(full(out.shape), full(out.shape)),
        compiler_params=pltpu.CompilerParams(vmem_limit_bytes=VMEM_LIMIT),
        cost_estimate=pl.CostEstimate(flops=10**6, bytes_accessed=3 * 2**20, transcendentals=0),
        name="edges",
    )(coef, fields, fields, before, after, kappa, kappa)


KEEP = STEPS + 1


def inner_kernel(coef, field, before, after, east_hbm, south_hbm, result, kept, field_v, east, south, one, two, scratch, sems):
    rows = field.shape[0]
    n_blocks = rows // 8
    loads = [pltpu.make_async_copy(field.at[pl.ds(8 * b, 8)], field_v.at[pl.ds(8 * b, 8)], sems.at[b]) for b in range(n_blocks)]
    faces_in = [pltpu.make_async_copy(east_hbm, east, sems.at[n_blocks]), pltpu.make_async_copy(south_hbm, south, sems.at[n_blocks + 1])]
    for copy in (*loads, *faces_in):
        copy.start()

    def block(b, carry):
        for q in range(8):
            row = b * 8 + q
            put_row(one, row, to_columns(mix_row(coef, row, field_v, before, after), scratch.at[q]))
        return carry

    for b in range(n_blocks):
        loads[b].wait()
    lax.fori_loop(0, n_blocks, block, 0)
    for copy in faces_in:
        copy.wait()
    for step in range(1, STEPS + 1):
        src, dst = (one, two) if step % 2 else (two, one)
        diffuse(src, dst, east, south, step, rows - 2 * step)
    last = one if STEPS % 2 == 0 else two

    keeps = [
        pltpu.make_async_copy(buffer.at[pl.ds(start, KEEP)], kept.at[at], sems.at[at])
        for at, (buffer, start) in enumerate(((one, 0), (two, 0), (one, rows - KEEP), (two, rows - KEEP)))
    ]
    for copy in keeps:
        copy.start()

    def back(b, carry):
        for q in range(8):
            row = b * 8 + q
            out = to_rows([last[row, i + 1] for i in range(NV)], scratch.at[q])
            for j in range(NV):
                field_v[row, :, pl.ds(LANES * j, LANES)] = out[j]
        return carry

    lax.fori_loop(0, n_blocks, back, 0)
    store = pltpu.make_async_copy(field_v.at[pl.ds(STEPS, rows - 2 * STEPS)], result.at[pl.ds(STEPS, rows - 2 * STEPS)], sems.at[4])
    store.start()
    for copy in (*keeps, store):
        copy.wait()


def inner(coef, fields, before, after, east, south):
    rows, slots, width = fields.shape
    vmem, hbm = pl.BlockSpec(memory_space=pltpu.VMEM), pl.BlockSpec(memory_space=pl.ANY)
    return pl.pallas_call(
        inner_kernel,
        out_shape=(
            jax.ShapeDtypeStruct(fields.shape, F32),
            jax.ShapeDtypeStruct((4, KEEP, GV, *TILE), F32),
        ),
        in_specs=[vmem, hbm, vmem, vmem, hbm, hbm],
        out_specs=(hbm, hbm),
        scratch_shapes=[
            pltpu.VMEM(fields.shape, F32),
            pltpu.VMEM(east.shape, F32),
            pltpu.VMEM(south.shape, F32),
            pltpu.VMEM((rows, GV, *TILE), F32),
            pltpu.VMEM((rows, GV, *TILE), F32),
            pltpu.VMEM((8, LANES, LANES), F32),
            pltpu.SemaphoreType.DMA((rows // 8 + 2,)),
        ],
        compiler_params=pltpu.CompilerParams(vmem_limit_bytes=VMEM_LIMIT),
        cost_estimate=pl.CostEstimate(flops=10**8, bytes_accessed=20 * 2**20, transcendentals=0),
        name="inner",
    )(coef, fields, before, after, east, south)


SPAN = 2 * STEPS + 1


def ends_kernel(inside, from_up, from_down, kappa_up, kappa_down, kept, east_hbm, south_hbm, partial, result, one, two, half, east, south, scratch, staged, sems):
    del partial
    rows = result.shape[0]
    upper, lower = 0, 1
    kept_in, faces_in = [], []
    for side in (upper, lower):
        own = STEPS if side == upper else 0
        first = 0 if side == upper else rows - KEEP
        pairs = ((kept.at[2 * side], one), (kept.at[2 * side + 1], two), (east_hbm.at[pl.ds(first, KEEP)], east), (south_hbm.at[pl.ds(first, KEEP)], south))
        for at, (src, dst) in enumerate(pairs):
            copy = pltpu.make_async_copy(src, dst.at[side, pl.ds(own, KEEP)], sems.at[4 * side + at])
            copy.start()
            (kept_in if at < 2 else faces_in).append(copy)
    for copy in (*kept_in, *faces_in):
        copy.wait()

    for side, halo, own_kappa in ((upper, from_up, kappa_up), (lower, from_down, kappa_down)):
        start = 0 if side == upper else KEEP
        for k in range(STEPS):
            put_row(one.at[side], start + k, to_columns([inside[side] * halo[k, :, pl.ds(LANES * j, LANES)] for j in range(NV)], scratch.at[k]))
        for k in range(STEPS + 1):
            is_own = k == STEPS if side == upper else k == 0
            if is_own:
                source, q = (own_kappa, 0) if side == upper else (own_kappa, 7)
            else:
                source, q = halo.at[STEPS], (k + 2 if side == upper else k - 1)
            factor = 0.5 if is_own else 0.5 * inside[side]
            spread = [jnp.broadcast_to(factor * source[q : q + 1, LANES * j : LANES * (j + 1)], TILE) for j in range(NV)]
            put_row(half, k, to_columns(spread, scratch.at[k]))
        if side == upper:
            coefficient_rows(half, east.at[side], south.at[side], 0, STEPS)
        else:
            for i in range(GV):
                half[STEPS + 1, i] = jnp.zeros(TILE, F32)
            for i in range(NV):
                south[side, STEPS, i] = half[0, i + 1] + half[1, i + 1]
            coefficient_rows(half, east.at[side], south.at[side], 1, STEPS, shift=STEPS)

    for step in range(1, STEPS + 1):
        src, dst = (one, two) if step % 2 else (two, one)
        keep_up, keep_down = inside[0], inside[1]
        diffuse(src.at[upper], dst.at[upper], east.at[upper], south.at[upper], step, STEPS, scale=lambda row: jnp.where(row < STEPS, keep_up, 1.0))
        diffuse(src.at[lower], dst.at[lower], east.at[lower], south.at[lower], SPAN - 1 - step - STEPS + 1, STEPS, scale=lambda row: jnp.where(row > STEPS, keep_down, 1.0))
    last = one if STEPS % 2 == 0 else two
    stores = []
    for side in (upper, lower):
        start = STEPS if side == upper else 1
        for k in range(STEPS):
            out = to_rows([last[side, start + k, i + 1] for i in range(NV)], scratch.at[k])
            for j in range(NV):
                staged[side, k, :, pl.ds(LANES * j, LANES)] = out[j]
        copy = pltpu.make_async_copy(staged.at[side], result.at[pl.ds(0 if side == upper else rows - STEPS, STEPS)], sems.at[side])
        copy.start()
        stores.append(copy)
    for copy in stores:
        copy.wait()


def ends(inside, from_up, from_down, kappa, kept, east, south, partial):
    rows, slots, width = partial.shape
    vmem, hbm = pl.BlockSpec(memory_space=pltpu.VMEM), pl.BlockSpec(memory_space=pl.ANY)
    return pl.pallas_call(
        ends_kernel,
        grid=(1,),
        out_shape=jax.ShapeDtypeStruct(partial.shape, F32),
        in_specs=[
            pl.BlockSpec(memory_space=pltpu.SMEM),
            vmem,
            vmem,
            pl.BlockSpec((8, width), lambda _: (0, 0)),
            pl.BlockSpec((8, width), lambda _: (rows // 8 - 1, 0)),
            hbm,
            hbm,
            hbm,
            hbm,
        ],
        out_specs=hbm,
        scratch_shapes=[
            pltpu.VMEM((2, SPAN, GV, *TILE), F32),
            pltpu.VMEM((2, SPAN, GV, *TILE), F32),
            pltpu.VMEM((STEPS + 2, GV, *TILE), F32),
            pltpu.VMEM((2, SPAN, NV + 1, *TILE), F32),
            pltpu.VMEM((2, SPAN, NV, *TILE), F32),
            pltpu.VMEM((8, LANES, LANES), F32),
            pltpu.VMEM((2, STEPS, slots, width), F32),
            pltpu.SemaphoreType.DMA((8,)),
        ],
        input_output_aliases={8: 0},
        compiler_params=pltpu.CompilerParams(vmem_limit_bytes=VMEM_LIMIT),
        cost_estimate=pl.CostEstimate(flops=10**7, bytes_accessed=8 * 2**20, transcendentals=0),
        name="ends",
    )(inside, from_up, from_down, kappa, kappa, kept, east, south, partial)


def ring(axis, step):
    size = lax.axis_size(axis)
    return [(i, (i + step) % size) for i in range(size)]


def local(forcing, kappa, diag_coef, lower_coef, upper_coef):
    slots = forcing.shape[1]
    tm, space = lax.axis_index("tm"), lax.axis_index("space")
    n_tm, n_space = lax.axis_size("tm"), lax.axis_size("space")
    down = jnp.where(tm == 0, 0.0, lower_coef[0]) * forcing[:, :1]
    up = jnp.where(tm == n_tm - 1, 0.0, upper_coef[slots - 1]) * forcing[:, slots - 1 :]
    after = lax.ppermute(down, "tm", ring("tm", -1))
    before = lax.ppermute(up, "tm", ring("tm", 1))
    east, south = faces(kappa)

    none = jnp.zeros((1,), F32)
    coef = jnp.stack([diag_coef, jnp.concatenate([lower_coef[1:], none]), jnp.concatenate([none, upper_coef[:-1]])])
    coef = jnp.broadcast_to(coef[:, :, None], (3, slots, LANES))
    inside = jnp.stack([jnp.where(space == 0, 0.0, 1.0), jnp.where(space == n_space - 1, 0.0, 1.0)]).astype(F32)

    to_up, to_down = edge_rows(coef, forcing, before, after, kappa)
    from_down = lax.ppermute(to_up, "space", ring("space", -1))
    from_up = lax.ppermute(to_down, "space", ring("space", 1))
    partial, kept = inner(coef, forcing, before, after, east, south)
    return ends(inside, from_up, from_down, kappa, kept, east, south, partial)


def solution(mesh):
    return jax.shard_map(
        local,
        mesh=mesh,
        in_specs=(P("space", "tm", None), P("space", None), P("tm"), P("tm"), P("tm")),
        out_specs=P("space", "tm", None),
        check_vma=False,
    )
```

```python
import jax
import jax.numpy as jnp
from jax import lax
from jax.experimental import pallas as pl
from jax.experimental.pallas import tpu as pltpu
from jax.sharding import PartitionSpec as P

STEPS = 6
NV = 16
LANES = 128
TILE = (8, LANES)
F32 = jnp.float32
GROUP = 4
BLOCK = 8
PAD = GROUP
FILL = 29 * 256
PARAMS = pltpu.CompilerParams(vmem_limit_bytes=62 * 2**20)
VMEM, HBM, SMEM = (pl.BlockSpec(memory_space=space) for space in (pltpu.VMEM, pltpu.HBM, pltpu.SMEM))


def cost(flops, mebibytes):
    return pl.CostEstimate(flops=flops, bytes_accessed=int(mebibytes * 2**20), transcendentals=0)


def iota(dim):
    return lax.broadcasted_iota(jnp.int32, TILE, dim)


def lanes(j):
    return pl.ds(LANES * j, LANES)


def tiles(*lead):
    return pltpu.VMEM((*lead, *TILE), F32)


def put_ghosts(rows, ghosts, start, count, batch=8):
    lane, slot = iota(1), iota(0)
    pending = []
    for first in range(0, count + batch, batch):
        made = []
        for k in range(first, min(first + batch, count)):
            west, east = pltpu.roll(rows[start + k, NV - 1], 1, 0), pltpu.roll(rows[start + k, 0], 7, 0)
            made.append((k, west, east, pltpu.roll(west, 8, 1), pltpu.roll(east, LANES - 8, 1)))
        for k, west, east, moved_west, moved_east in pending:
            ghosts[start + k, 0] = jnp.where(slot == 0, jnp.where(lane >= 8, moved_west, 0.0), west)
            ghosts[start + k, 1] = jnp.where(slot == 7, jnp.where(lane < LANES - 8, moved_east, 0.0), east)
        pending = made


def to_columns(natural, scratch):
    scratch[...] = jnp.concatenate(natural, axis=0).T


def from_columns(scratch, rows, row):
    for i in range(NV):
        rows[row, i] = scratch[pl.ds(i, 8, stride=NV), :]


def transpose_in(natural, rows, scratch, first, n_blocks, arrive):
    def iteration(b, stages):
        if 1 in stages:
            for q in range(BLOCK):
                from_columns(scratch.at[(b - 1) & 1, q], rows, first + (b - 1) * BLOCK + q)
        if 0 in stages:
            for q in range(BLOCK):
                to_columns(natural(b * BLOCK + q), scratch.at[b & 1, q])

    def body(b, carry):
        iteration(b, (0, 1))
        return carry

    done = 0
    for upto, ready in arrive:
        ready()
        if done == 0:
            iteration(0, (0,))
            done = 1
        lax.fori_loop(done, upto, body, 0)
        done = upto
    iteration(n_blocks, (1,))


def transpose_out(rows, scratch, starts, put):
    for b in range(len(starts) + 1):
        if b > 0:
            for q in range(BLOCK):
                flipped = scratch[(b - 1) & 1, q].T
                put(b - 1, q, [flipped[8 * j : 8 * j + 8] for j in range(NV)])
        if b < len(starts):
            for q in range(BLOCK):
                for i in range(NV):
                    scratch[b & 1, q, pl.ds(i, 8, stride=NV), :] = rows[starts[b] + q, i]


def face_row(half, half_ghosts, east, south, row, shift, with_south=True):
    here = [half_ghosts[row, 0], *[half[row, i] for i in range(NV)], half_ghosts[row, 1]]
    for i in range(NV + 1):
        east[row + shift, i] = here[i] + here[i + 1]
    if with_south:
        for i in range(NV):
            south[row + shift, i] = here[i + 1] + half[row + 1, i]


def diffuse(src, src_ghosts, dst, dst_ghosts, east, south, lo, count):
    def group(k, carry):
        base = lo + k * GROUP
        v, north = carry[:NV], carry[NV:]
        for q in range(GROUP):
            row = base + q
            below = [src[row + 1, i] for i in range(NV)]
            west = east[row, 0] * (v[0] - src_ghosts[row, 0])
            flux = []
            for i in range(NV):
                v_east = v[i + 1] if i + 1 < NV else src_ghosts[row, 1]
                here = east[row, i + 1] * (v_east - v[i])
                under = south[row, i] * (below[i] - v[i])
                dst[row, i] = (v[i] + (here - west)) + (under - north[i])
                west = here
                flux.append(under)
            v, north = below, flux
        return (*v, *north)

    v = [src[lo, i] for i in range(NV)]
    north = [south[lo - 1, i] * (v[i] - src[lo - 1, i]) for i in range(NV)]
    lax.fori_loop(0, count // GROUP, group, (*v, *north))
    put_ghosts(dst, dst_ghosts, lo, count)


def all_steps(one, two, east, south, first, rows, after_step=None):
    for step in range(1, STEPS + 1):
        src, dst = (one, two) if step % 2 else (two, one)
        count = -(-(rows - 2 * step) // GROUP) * GROUP
        diffuse(*src, *dst, east, south, first + step, count)
        if after_step is not None and step < STEPS:
            after_step(dst)


def own_coef(diag, lower, upper):
    slot, slots = iota(0), diag.shape[0]
    made = []
    for ref, shift in ((diag, 0), (lower, 1), (upper, -1)):
        value = jnp.zeros(TILE, F32)
        for t in range(slots):
            if 0 <= t + shift < slots:
                value = jnp.where(slot == t, ref[t + shift], value)
        made.append(value)
    return made


def edge_scales(lower, upper):
    tm, groups = lax.axis_index("tm"), lax.axis_size("tm")
    slots = lower.shape[0]
    return jnp.where(tm == groups - 1, 0.0, upper[slots - 1]), jnp.where(tm == 0, 0.0, lower[0])


class Copies:
    def __init__(self, sems):
        self.sems, self.used = sems, 0

    def start(self, src, dst):
        made = pltpu.make_async_copy(src, dst, self.sems.at[self.used])
        self.used += 1
        made.start()
        return made


def wait(copies):
    for made in copies:
        made.wait()


KAPPA, PACK = STEPS, STEPS + 1


def packs_kernel(field, kappa, go, pack_up, pack_down, field_v, kappa_v, sems):
    del go
    rows = field.shape[0]
    copies = Copies(sems)
    sides = ((pack_up, 0, 0), (pack_down, rows - STEPS, rows - 8))
    loads = [
        [copies.start(field.at[pl.ds(start, STEPS)], field_v.at[side]), copies.start(kappa.at[pl.ds(tile, 8)], kappa_v.at[side])]
        for side, (_, start, tile) in enumerate(sides)
    ]
    stores = []
    for side, (pack, _, _) in enumerate(sides):
        wait(loads[side])
        stores += [copies.start(field_v.at[side], pack.at[pl.ds(0, STEPS)]), copies.start(kappa_v.at[side], pack.at[KAPPA])]
    wait(stores)


def packs(fields, kappa, go):
    _, slots, width = fields.shape
    pack = jax.ShapeDtypeStruct((PACK, slots, width), F32)
    return pl.pallas_call(
        packs_kernel,
        out_shape=(pack, pack),
        in_specs=[HBM, HBM, HBM],
        out_specs=(HBM, HBM),
        scratch_shapes=[pltpu.VMEM((2, STEPS, slots, width), F32), pltpu.VMEM((2, 8, width), F32), pltpu.SemaphoreType.DMA((8,))],
        compiler_params=PARAMS,
        cost_estimate=cost(10**5, 2),
        name="packs",
    )(fields, kappa, go)


def pick_kernel(lower, upper, field, up, down, field_v, up_v, down_v, sems):
    rows = field.shape[0]
    copies = Copies(sems)
    cuts = [rows * k // 4 for k in range(5)]
    parts = [pl.ds(a, b - a) for a, b in zip(cuts[:-1], cuts[1:], strict=True)]
    loads = [copies.start(field.at[part], field_v.at[part]) for part in parts]
    up_scale, down_scale = edge_scales(lower, upper)
    stores = []

    def body(row, carry):
        up_v[row] = up_scale * field_v[row, 7:8, :]
        down_v[row] = down_scale * field_v[row, 0:1, :]
        return carry

    for part, load in zip(parts, loads, strict=True):
        load.wait()
        lax.fori_loop(part.start, part.start + part.size, body, 0, unroll=2)
        stores += [copies.start(up_v.at[part], up.at[part]), copies.start(down_v.at[part], down.at[part])]
    wait(stores)


def pick(lower, upper, fields):
    rows, slots, width = fields.shape
    edge = jax.ShapeDtypeStruct((rows, 1, width), F32)
    return pl.pallas_call(
        pick_kernel,
        out_shape=(edge, edge),
        in_specs=[SMEM, SMEM, HBM],
        out_specs=(HBM, HBM),
        scratch_shapes=[
            pltpu.VMEM(fields.shape, F32),
            pltpu.VMEM(edge.shape, F32),
            pltpu.VMEM(edge.shape, F32),
            pltpu.SemaphoreType.DMA((12,)),
        ],
        compiler_params=PARAMS,
        cost_estimate=cost(10**6, 5),
        name="pick",
    )(lower, upper, fields)


def faces_kernel(kappa, east_out, south_out, half, ghosts, east, south, scratch, sems):
    rows = kappa.shape[0]
    n_blocks = rows // BLOCK
    copies = Copies(sems)
    stores = []
    for i in range(NV):
        half[rows, i] = jnp.zeros(TILE, F32)
    for b in range(n_blocks + 1):
        if b >= 1:
            for q in range(BLOCK):
                from_columns(scratch.at[(b - 1) & 1, q], half, (b - 1) * BLOCK + q)
        if b < n_blocks:
            for q in range(BLOCK):
                row = b * BLOCK + q
                to_columns([jnp.broadcast_to(0.5 * kappa[row : row + 1, lanes(j)], TILE) for j in range(NV)], scratch.at[b & 1, q])
    put_ghosts(half, ghosts, 0, rows)
    for b in range(n_blocks):
        for q in range(BLOCK):
            face_row(half, ghosts, east, south, b * BLOCK + q, 0)
        at = pl.ds(b * BLOCK, BLOCK)
        stores += [copies.start(east.at[at], east_out.at[at]), copies.start(south.at[at], south_out.at[at])]
    wait(stores)


def faces(kappa):
    rows = kappa.shape[0]
    return pl.pallas_call(
        faces_kernel,
        out_shape=(jax.ShapeDtypeStruct((rows, NV + 1, *TILE), F32), jax.ShapeDtypeStruct((rows, NV, *TILE), F32)),
        in_specs=[VMEM],
        out_specs=(HBM, HBM),
        scratch_shapes=[
            tiles(rows + 1, NV),
            tiles(rows, 2),
            tiles(rows, NV + 1),
            tiles(rows, NV),
            pltpu.VMEM((2, BLOCK, LANES, LANES), F32),
            pltpu.SemaphoreType.DMA((2 * (rows // BLOCK),)),
        ],
        compiler_params=PARAMS,
        cost_estimate=cost(2 * 10**7, 9),
        name="faces",
    )(kappa)


def state(rows):
    return [tiles(rows, NV), tiles(rows, 2), tiles(rows, NV), tiles(rows, 2), tiles(rows, NV + 1), tiles(rows, NV)]


def mix(coef, x, before, after):
    slot = iota(0)
    later = jnp.where(slot == 7, jnp.broadcast_to(after, TILE), coef[1] * pltpu.roll(x, 7, 0))
    earlier = jnp.where(slot == 0, jnp.broadcast_to(before, TILE), coef[2] * pltpu.roll(x, 1, 0))
    return coef[0] * x + later + earlier


def corners_kernel(before, after, go, first, last, first_v, last_v, sems):
    del go
    rows = before.shape[0]
    copies = Copies(sems)
    loads, stores = [], []
    for held, start in ((first_v, 0), (last_v, rows - STEPS)):
        loads.append([copies.start(src.at[pl.ds(start, STEPS)], held.at[pl.ds(STEPS * k, STEPS)]) for k, src in enumerate((before, after))])
    for load, held, out in zip(loads, (first_v, last_v), (first, last), strict=True):
        wait(load)
        stores.append(copies.start(held, out))
    wait(stores)


def corners(before, after, go):
    edge = jax.ShapeDtypeStruct((2 * STEPS, *before.shape[1:]), F32)
    held = pltpu.VMEM(edge.shape, F32)
    return pl.pallas_call(
        corners_kernel,
        out_shape=(edge, edge),
        in_specs=[HBM, HBM, HBM],
        out_specs=(HBM, HBM),
        scratch_shapes=[held, held, pltpu.SemaphoreType.DMA((6,))],
        compiler_params=PARAMS,
        cost_estimate=cost(10**5, 1),
        name="corners",
    )(before, after, go)


def slab_kernel(diag, lower, upper, field, kappa, before, after, from_up, from_down, far_up, far_down, east_own, south_own, result, field_v, before_v, after_v, far_v, kappa_v, half, half_ghosts, one, one_g, two, two_g, east, south, scratch, sems, fill):
    total = field.shape[0]
    span = total + 2 * STEPS
    fill[0] = jnp.zeros(TILE, F32)
    fill[FILL - 1] = jnp.zeros(TILE, F32)
    copies = Copies(sems)
    kappa_in = []
    for at, (src, row) in enumerate(((from_up.at[KAPPA], None), (kappa, 0), (kappa, total - 8), (from_down.at[KAPPA], None))):
        kappa_in.append(copies.start(src if row is None else src.at[pl.ds(row, 8)], kappa_v.at[pl.ds(8 * at, 8)]))
    halo_in = [
        copies.start(from_up.at[pl.ds(0, STEPS)], field_v.at[pl.ds(total, STEPS)]),
        copies.start(from_down.at[pl.ds(0, STEPS)], field_v.at[pl.ds(total + STEPS, STEPS)]),
        copies.start(far_up, far_v.at[0]),
        copies.start(far_down, far_v.at[1]),
    ]
    quarter = total // 4
    field_in = []
    for k in range(4):
        at = pl.ds(k * quarter, quarter)
        field_in.append([copies.start(src.at[at], dst.at[at]) for src, dst in ((field, field_v), (before, before_v), (after, after_v))])
    faces_in = [
        copies.start(east_own, east.at[pl.ds(STEPS, total)]),
        copies.start(south_own.at[pl.ds(0, total - 1)], south.at[pl.ds(STEPS, total - 1)]),
    ]
    space, slabs = lax.axis_index("space"), lax.axis_size("space")
    at_top, at_bottom = space == 0, space == slabs - 1
    coef = own_coef(diag, lower, upper)

    wait(kappa_in)
    for edge, start in ((at_top, 0), (at_bottom, 24)):

        @pl.when(edge)
        def _(start=start):
            kappa_v[pl.ds(start, 8), :] = jnp.zeros((8, kappa_v.shape[1]), F32)

    sources = [*range(2, 9), *range(23, 30)]
    for k, row in enumerate(sources):
        spread = [jnp.broadcast_to(0.5 * kappa_v[row : row + 1, lanes(j)], TILE) for j in range(NV)]
        to_columns(spread, scratch.at[k // BLOCK, k % BLOCK])
    for k in range(len(sources)):
        from_columns(scratch.at[k // BLOCK, k % BLOCK], half, k)
    put_ghosts(half, half_ghosts, 0, len(sources))
    own_end = STEPS + total
    for k in range(STEPS):
        face_row(half, half_ghosts, east, south, k, 0)
        face_row(half, half_ghosts, east, south, STEPS + 2 + k, own_end - STEPS - 2, with_south=k < STEPS - 1)
    for i in range(NV):
        south[own_end - 1, i] = half[STEPS + 1, i] + half[STEPS + 2, i]

    wait(halo_in)
    for k in range(2 * STEPS):
        side, q = divmod(k, STEPS)
        near = [far_v[side, q], far_v[side, STEPS + q]]
        halo = [mix(coef, field_v[total + k, :, lanes(j)], *[x[:, LANES * j : LANES * (j + 1)] for x in near]) for j in range(NV)]
        to_columns(halo, scratch.at[k // BLOCK, k % BLOCK])
    for k in range(2 * STEPS):
        from_columns(scratch.at[k // BLOCK, k % BLOCK], one, k if k < STEPS else own_end + k - STEPS)

    def mixed(row):
        return [mix(coef, field_v[row, :, lanes(j)], before_v[row, :, lanes(j)], after_v[row, :, lanes(j)]) for j in range(NV)]

    arrive = [((k + 1) * quarter // BLOCK, lambda k=k: wait(field_in[k])) for k in range(4)]
    transpose_in(mixed, one, scratch, STEPS, total // BLOCK, arrive)
    put_ghosts(one, one_g, 0, span)

    def clear(state):
        rows, ghosts = state
        for edge, start in ((at_top, 0), (at_bottom, own_end)):

            @pl.when(edge)
            def _(start=start):
                for k in range(STEPS):
                    for i in range(NV):
                        rows[start + k, i] = jnp.zeros(TILE, F32)
                    ghosts[start + k, 0] = jnp.zeros(TILE, F32)
                    ghosts[start + k, 1] = jnp.zeros(TILE, F32)

    clear((one, one_g))
    wait(faces_in)
    all_steps((one, one_g), (two, two_g), east, south, 0, span, clear)
    stores = []

    def put(b, q, vregs):
        row = b * BLOCK + q
        for j, v in enumerate(vregs):
            field_v[row, :, lanes(j)] = v
        if q == BLOCK - 1:
            at = pl.ds(b * BLOCK, BLOCK)
            stores.append(copies.start(field_v.at[at], result.at[at]))

    transpose_out(one, scratch, list(range(STEPS, own_end, BLOCK)), put)
    wait(stores)


def slab(diag, lower, upper, fields, kappa, before, after, from_up, from_down, far_up, far_down, east, south):
    rows, slots, width = fields.shape
    span = rows + 2 * STEPS
    edge = pltpu.VMEM(before.shape, F32)
    return pl.pallas_call(
        slab_kernel,
        out_shape=jax.ShapeDtypeStruct(fields.shape, F32),
        in_specs=[SMEM, SMEM, SMEM, *[HBM] * 10],
        out_specs=HBM,
        scratch_shapes=[
            pltpu.VMEM((span, slots, width), F32),
            edge,
            edge,
            pltpu.VMEM((2, *far_up.shape), F32),
            pltpu.VMEM((32, width), F32),
            tiles(2 * STEPS + 3, NV),
            tiles(2 * STEPS + 2, 2),
            *state(span + 2 * PAD),
            pltpu.VMEM((2, BLOCK, LANES, LANES), F32),
            pltpu.SemaphoreType.DMA((32,)),
            tiles(FILL),
        ],
        compiler_params=PARAMS,
        cost_estimate=cost(4 * 10**8, 16),
        name="slab",
    )(diag, lower, upper, fields, kappa, before, after, from_up, from_down, far_up, far_down, east, south)


def ring(axis, step):
    size = lax.axis_size(axis)
    return [(i, (i + step) % size) for i in range(size)]


def local(forcing, kappa, diag, lower, upper):
    up, down = pick(lower, upper, forcing)
    before = lax.ppermute(up, "tm", ring("tm", 1))
    after = lax.ppermute(down, "tm", ring("tm", -1))
    pack_up, pack_down = packs(forcing, kappa, down)
    from_down = lax.ppermute(pack_up, "space", ring("space", -1))
    from_up = lax.ppermute(pack_down, "space", ring("space", 1))
    east, south = faces(kappa)
    first, last = corners(before, after, east)
    far_down = lax.ppermute(first, "space", ring("space", -1))
    far_up = lax.ppermute(last, "space", ring("space", 1))
    return slab(diag, lower, upper, forcing, kappa, before, after, from_up, from_down, far_up, far_down, east, south)


def solution(mesh):
    return jax.shard_map(
        local,
        mesh=mesh,
        in_specs=(P("space", "tm", None), P("space", None), P("tm"), P("tm"), P("tm")),
        out_specs=P("space", "tm", None),
        check_vma=False,
    )
```

```python
import jax
import jax.numpy as jnp
from jax import lax
from jax.experimental import pallas as pl
from jax.experimental.pallas import tpu as pltpu
from jax.sharding import PartitionSpec as P

STEPS = 6
NV = 16
LANES = 128
TILE = (8, LANES)
F32 = jnp.float32
GROUP = 4
BLOCK = 8
PAD = GROUP
FILL = 32 * 256
MORE = 62 * 256
PARAMS = pltpu.CompilerParams(vmem_limit_bytes=63 * 2**20 + 2**19)
VMEM, HBM, SMEM = (pl.BlockSpec(memory_space=space) for space in (pltpu.VMEM, pltpu.HBM, pltpu.SMEM))


def cost(flops, mebibytes):
    return pl.CostEstimate(flops=flops, bytes_accessed=int(mebibytes * 2**20), transcendentals=0)


def iota(dim):
    return lax.broadcasted_iota(jnp.int32, TILE, dim)


def lanes(j):
    return pl.ds(LANES * j, LANES)


def tiles(*lead):
    return pltpu.VMEM((*lead, *TILE), F32)


def put_ghosts(rows, ghosts, start, count, batch=8):
    lane, slot = iota(1), iota(0)
    pending = []
    for first in range(0, count + batch, batch):
        made = []
        for k in range(first, min(first + batch, count)):
            west, east = pltpu.roll(rows[start + k, NV - 1], 1, 0), pltpu.roll(rows[start + k, 0], 7, 0)
            made.append((k, west, east, pltpu.roll(west, 8, 1), pltpu.roll(east, LANES - 8, 1)))
        for k, west, east, moved_west, moved_east in pending:
            ghosts[start + k, 0] = jnp.where(slot == 0, jnp.where(lane >= 8, moved_west, 0.0), west)
            ghosts[start + k, 1] = jnp.where(slot == 7, jnp.where(lane < LANES - 8, moved_east, 0.0), east)
        pending = made


def to_columns(natural, scratch):
    scratch[...] = jnp.concatenate(natural, axis=0).T


def from_columns(scratch, rows, row):
    for i in range(NV):
        rows[row, i] = scratch[pl.ds(i, 8, stride=NV), :]


def transpose_in(natural, rows, scratch, first, n_blocks, arrive):
    def iteration(b, stages):
        if 1 in stages:
            for q in range(BLOCK):
                from_columns(scratch.at[(b - 1) & 1, q], rows, first + (b - 1) * BLOCK + q)
        if 0 in stages:
            for q in range(BLOCK):
                to_columns(natural(b * BLOCK + q), scratch.at[b & 1, q])

    def body(b, carry):
        iteration(b, (0, 1))
        return carry

    done = 0
    for upto, ready in arrive:
        ready()
        if done == 0:
            iteration(0, (0,))
            done = 1
        lax.fori_loop(done, upto, body, 0)
        done = upto
    iteration(n_blocks, (1,))


def transpose_out(rows, scratch, starts, put):
    for b in range(len(starts) + 1):
        if b > 0:
            for q in range(BLOCK):
                flipped = scratch[(b - 1) & 1, q].T
                put(b - 1, q, [flipped[8 * j : 8 * j + 8] for j in range(NV)])
        if b < len(starts):
            for q in range(BLOCK):
                for i in range(NV):
                    scratch[b & 1, q, pl.ds(i, 8, stride=NV), :] = rows[starts[b] + q, i]


def face_row(half, half_ghosts, east, south, row, shift, with_south=True):
    here = [half_ghosts[row, 0], *[half[row, i] for i in range(NV)], half_ghosts[row, 1]]
    for i in range(NV + 1):
        east[row + shift, i] = here[i] + here[i + 1]
    if with_south:
        for i in range(NV):
            south[row + shift, i] = here[i + 1] + half[row + 1, i]


def diffuse(src, src_ghosts, dst, dst_ghosts, east, south, lo, count):
    def group(k, carry):
        base = lo + k * GROUP
        v, north = carry[:NV], carry[NV:]
        for q in range(GROUP):
            row = base + q
            below = [src[row + 1, i] for i in range(NV)]
            west = east[row, 0] * (v[0] - src_ghosts[row, 0])
            flux = []
            for i in range(NV):
                v_east = v[i + 1] if i + 1 < NV else src_ghosts[row, 1]
                here = east[row, i + 1] * (v_east - v[i])
                under = south[row, i] * (below[i] - v[i])
                dst[row, i] = (v[i] + (here - west)) + (under - north[i])
                west = here
                flux.append(under)
            v, north = below, flux
        return (*v, *north)

    v = [src[lo, i] for i in range(NV)]
    north = [south[lo - 1, i] * (v[i] - src[lo - 1, i]) for i in range(NV)]
    lax.fori_loop(0, count // GROUP, group, (*v, *north))
    put_ghosts(dst, dst_ghosts, lo, count)


def all_steps(one, two, east, south, first, rows, after_step=None):
    for step in range(1, STEPS + 1):
        src, dst = (one, two) if step % 2 else (two, one)
        count = -(-(rows - 2 * step) // GROUP) * GROUP
        diffuse(*src, *dst, east, south, first + step, count)
        if after_step is not None and step < STEPS:
            after_step(dst)


def own_coef(diag, lower, upper):
    slot, slots = iota(0), diag.shape[0]
    made = []
    for ref, shift in ((diag, 0), (lower, 1), (upper, -1)):
        value = jnp.zeros(TILE, F32)
        for t in range(slots):
            if 0 <= t + shift < slots:
                value = jnp.where(slot == t, ref[t + shift], value)
        made.append(value)
    return made


def edge_scales(lower, upper):
    tm, groups = lax.axis_index("tm"), lax.axis_size("tm")
    slots = lower.shape[0]
    return jnp.where(tm == groups - 1, 0.0, upper[slots - 1]), jnp.where(tm == 0, 0.0, lower[0])


class Copies:
    def __init__(self, sems):
        self.sems, self.used = sems, 0

    def start(self, src, dst):
        made = pltpu.make_async_copy(src, dst, self.sems.at[self.used])
        self.used += 1
        made.start()
        return made


def wait(copies):
    for made in copies:
        made.wait()


KAPPA, PACK = STEPS, STEPS + 1


def packs_kernel(field, kappa, go, pack_up, pack_down, field_v, kappa_v, sems):
    del go
    rows = field.shape[0]
    copies = Copies(sems)
    sides = ((pack_up, 0, 0), (pack_down, rows - STEPS, rows - 8))
    loads = [
        [copies.start(field.at[pl.ds(start, STEPS)], field_v.at[side]), copies.start(kappa.at[pl.ds(tile, 8)], kappa_v.at[side])]
        for side, (_, start, tile) in enumerate(sides)
    ]
    stores = []
    for side, (pack, _, _) in enumerate(sides):
        wait(loads[side])
        stores += [copies.start(field_v.at[side], pack.at[pl.ds(0, STEPS)]), copies.start(kappa_v.at[side], pack.at[KAPPA])]
    wait(stores)


def packs(fields, kappa, go):
    _, slots, width = fields.shape
    pack = jax.ShapeDtypeStruct((PACK, slots, width), F32)
    return pl.pallas_call(
        packs_kernel,
        out_shape=(pack, pack),
        in_specs=[HBM, HBM, HBM],
        out_specs=(HBM, HBM),
        scratch_shapes=[pltpu.VMEM((2, STEPS, slots, width), F32), pltpu.VMEM((2, 8, width), F32), pltpu.SemaphoreType.DMA((8,))],
        compiler_params=PARAMS,
        cost_estimate=cost(10**5, 2),
        name="packs",
    )(fields, kappa, go)


def pick_kernel(lower, upper, field, up, down, field_v, up_v, down_v, sems):
    rows = field.shape[0]
    copies = Copies(sems)
    cuts = [rows * k // 4 for k in range(5)]
    parts = [pl.ds(a, b - a) for a, b in zip(cuts[:-1], cuts[1:], strict=True)]
    loads = [copies.start(field.at[part], field_v.at[part]) for part in parts]
    up_scale, down_scale = edge_scales(lower, upper)
    stores = []

    def body(row, carry):
        up_v[row] = up_scale * field_v[row, 7:8, :]
        down_v[row] = down_scale * field_v[row, 0:1, :]
        return carry

    for part, load in zip(parts, loads, strict=True):
        load.wait()
        lax.fori_loop(part.start, part.start + part.size, body, 0, unroll=2)
        stores += [copies.start(up_v.at[part], up.at[part]), copies.start(down_v.at[part], down.at[part])]
    wait(stores)


def pick(lower, upper, fields):
    rows, slots, width = fields.shape
    edge = jax.ShapeDtypeStruct((rows, 1, width), F32)
    return pl.pallas_call(
        pick_kernel,
        out_shape=(edge, edge),
        in_specs=[SMEM, SMEM, HBM],
        out_specs=(HBM, HBM),
        scratch_shapes=[
            pltpu.VMEM(fields.shape, F32),
            pltpu.VMEM(edge.shape, F32),
            pltpu.VMEM(edge.shape, F32),
            pltpu.SemaphoreType.DMA((12,)),
        ],
        compiler_params=PARAMS,
        cost_estimate=cost(10**6, 5),
        name="pick",
    )(lower, upper, fields)


def faces_kernel(kappa, east_out, south_out, half, ghosts, east, south, scratch, sems):
    rows = kappa.shape[0]
    n_blocks = rows // BLOCK
    copies = Copies(sems)
    stores = []
    for i in range(NV):
        half[rows, i] = jnp.zeros(TILE, F32)
    for b in range(n_blocks + 1):
        if b >= 1:
            for q in range(BLOCK):
                from_columns(scratch.at[(b - 1) & 1, q], half, (b - 1) * BLOCK + q)
        if b < n_blocks:
            for q in range(BLOCK):
                row = b * BLOCK + q
                to_columns([jnp.broadcast_to(0.5 * kappa[row : row + 1, lanes(j)], TILE) for j in range(NV)], scratch.at[b & 1, q])
    put_ghosts(half, ghosts, 0, rows)
    for b in range(n_blocks):
        for q in range(BLOCK):
            face_row(half, ghosts, east, south, b * BLOCK + q, 0)
        at = pl.ds(b * BLOCK, BLOCK)
        stores += [copies.start(east.at[at], east_out.at[at]), copies.start(south.at[at], south_out.at[at])]
    wait(stores)


def faces(kappa):
    rows = kappa.shape[0]
    return pl.pallas_call(
        faces_kernel,
        out_shape=(jax.ShapeDtypeStruct((rows, NV + 1, *TILE), F32), jax.ShapeDtypeStruct((rows, NV, *TILE), F32)),
        in_specs=[VMEM],
        out_specs=(HBM, HBM),
        scratch_shapes=[
            tiles(rows + 1, NV),
            tiles(rows, 2),
            tiles(rows, NV + 1),
            tiles(rows, NV),
            pltpu.VMEM((2, BLOCK, LANES, LANES), F32),
            pltpu.SemaphoreType.DMA((2 * (rows // BLOCK),)),
        ],
        compiler_params=PARAMS,
        cost_estimate=cost(2 * 10**7, 9),
        name="faces",
    )(kappa)


def state(rows):
    return [tiles(rows, NV), tiles(rows, 2), tiles(rows, NV), tiles(rows, 2), tiles(rows, NV + 1), tiles(rows, NV)]


def mix(coef, x, before, after):
    slot = iota(0)
    later = jnp.where(slot == 7, jnp.broadcast_to(after, TILE), coef[1] * pltpu.roll(x, 7, 0))
    earlier = jnp.where(slot == 0, jnp.broadcast_to(before, TILE), coef[2] * pltpu.roll(x, 1, 0))
    return coef[0] * x + later + earlier


def corners_kernel(before, after, go, first, last, first_v, last_v, sems, fill):
    del go
    fill[0] = jnp.zeros(TILE, F32)
    fill[MORE - 1] = jnp.zeros(TILE, F32)
    rows = before.shape[0]
    copies = Copies(sems)
    loads, stores = [], []
    for held, start in ((first_v, 0), (last_v, rows - STEPS)):
        loads.append([copies.start(src.at[pl.ds(start, STEPS)], held.at[pl.ds(STEPS * k, STEPS)]) for k, src in enumerate((before, after))])
    for load, held, out in zip(loads, (first_v, last_v), (first, last), strict=True):
        wait(load)
        stores.append(copies.start(held, out))
    wait(stores)


def corners(before, after, go):
    edge = jax.ShapeDtypeStruct((2 * STEPS, *before.shape[1:]), F32)
    held = pltpu.VMEM(edge.shape, F32)
    return pl.pallas_call(
        corners_kernel,
        out_shape=(edge, edge),
        in_specs=[HBM, HBM, HBM],
        out_specs=(HBM, HBM),
        scratch_shapes=[held, held, pltpu.SemaphoreType.DMA((6,)), tiles(MORE)],
        compiler_params=PARAMS,
        cost_estimate=cost(10**5, 1),
        name="corners",
    )(before, after, go)


def slab_kernel(diag, lower, upper, field, kappa, before, after, from_up, from_down, far_up, far_down, east_own, south_own, result, field_v, before_v, after_v, far_v, kappa_v, half, half_ghosts, one, one_g, two, two_g, east, south, scratch, sems, fill):
    total = field.shape[0]
    span = total + 2 * STEPS
    fill[0] = jnp.zeros(TILE, F32)
    fill[FILL - 1] = jnp.zeros(TILE, F32)
    copies = Copies(sems)
    kappa_in = []
    for at, (src, row) in enumerate(((from_up.at[KAPPA], None), (kappa, 0), (kappa, total - 8), (from_down.at[KAPPA], None))):
        kappa_in.append(copies.start(src if row is None else src.at[pl.ds(row, 8)], kappa_v.at[pl.ds(8 * at, 8)]))
    halo_in = [
        copies.start(from_up.at[pl.ds(0, STEPS)], field_v.at[pl.ds(total, STEPS)]),
        copies.start(from_down.at[pl.ds(0, STEPS)], field_v.at[pl.ds(total + STEPS, STEPS)]),
        copies.start(far_up, far_v.at[0]),
        copies.start(far_down, far_v.at[1]),
    ]
    quarter = total // 4
    field_in = []
    for k in range(4):
        at = pl.ds(k * quarter, quarter)
        field_in.append([copies.start(src.at[at], dst.at[at]) for src, dst in ((field, field_v), (before, before_v), (after, after_v))])
    faces_in = [
        copies.start(east_own, east.at[pl.ds(STEPS, total)]),
        copies.start(south_own.at[pl.ds(0, total - 1)], south.at[pl.ds(STEPS, total - 1)]),
    ]
    space, slabs = lax.axis_index("space"), lax.axis_size("space")
    at_top, at_bottom = space == 0, space == slabs - 1
    coef = own_coef(diag, lower, upper)

    wait(kappa_in)
    for edge, start in ((at_top, 0), (at_bottom, 24)):

        @pl.when(edge)
        def _(start=start):
            kappa_v[pl.ds(start, 8), :] = jnp.zeros((8, kappa_v.shape[1]), F32)

    sources = [*range(2, 9), *range(23, 30)]
    for k, row in enumerate(sources):
        spread = [jnp.broadcast_to(0.5 * kappa_v[row : row + 1, lanes(j)], TILE) for j in range(NV)]
        to_columns(spread, scratch.at[k // BLOCK, k % BLOCK])
    for k in range(len(sources)):
        from_columns(scratch.at[k // BLOCK, k % BLOCK], half, k)
    put_ghosts(half, half_ghosts, 0, len(sources))
    own_end = STEPS + total
    for k in range(STEPS):
        face_row(half, half_ghosts, east, south, k, 0)
        face_row(half, half_ghosts, east, south, STEPS + 2 + k, own_end - STEPS - 2, with_south=k < STEPS - 1)
    for i in range(NV):
        south[own_end - 1, i] = half[STEPS + 1, i] + half[STEPS + 2, i]

    wait(halo_in)
    for k in range(2 * STEPS):
        side, q = divmod(k, STEPS)
        near = [far_v[side, q], far_v[side, STEPS + q]]
        halo = [mix(coef, field_v[total + k, :, lanes(j)], *[x[:, LANES * j : LANES * (j + 1)] for x in near]) for j in range(NV)]
        to_columns(halo, scratch.at[k // BLOCK, k % BLOCK])
    for k in range(2 * STEPS):
        from_columns(scratch.at[k // BLOCK, k % BLOCK], one, k if k < STEPS else own_end + k - STEPS)

    def mixed(row):
        return [mix(coef, field_v[row, :, lanes(j)], before_v[row, :, lanes(j)], after_v[row, :, lanes(j)]) for j in range(NV)]

    arrive = [((k + 1) * quarter // BLOCK, lambda k=k: wait(field_in[k])) for k in range(4)]
    transpose_in(mixed, one, scratch, STEPS, total // BLOCK, arrive)
    put_ghosts(one, one_g, 0, span)

    def clear(state):
        rows, ghosts = state
        for edge, start in ((at_top, 0), (at_bottom, own_end)):

            @pl.when(edge)
            def _(start=start):
                for k in range(STEPS):
                    for i in range(NV):
                        rows[start + k, i] = jnp.zeros(TILE, F32)
                    ghosts[start + k, 0] = jnp.zeros(TILE, F32)
                    ghosts[start + k, 1] = jnp.zeros(TILE, F32)

    clear((one, one_g))
    wait(faces_in)
    all_steps((one, one_g), (two, two_g), east, south, 0, span, clear)
    stores = []

    def put(b, q, vregs):
        row = b * BLOCK + q
        for j, v in enumerate(vregs):
            field_v[row, :, lanes(j)] = v
        if q == BLOCK - 1:
            at = pl.ds(b * BLOCK, BLOCK)
            stores.append(copies.start(field_v.at[at], result.at[at]))

    transpose_out(one, scratch, list(range(STEPS, own_end, BLOCK)), put)
    wait(stores)


def slab(diag, lower, upper, fields, kappa, before, after, from_up, from_down, far_up, far_down, east, south):
    rows, slots, width = fields.shape
    span = rows + 2 * STEPS
    edge = pltpu.VMEM(before.shape, F32)
    return pl.pallas_call(
        slab_kernel,
        out_shape=jax.ShapeDtypeStruct(fields.shape, F32),
        in_specs=[SMEM, SMEM, SMEM, *[HBM] * 10],
        out_specs=HBM,
        scratch_shapes=[
            pltpu.VMEM((span, slots, width), F32),
            edge,
            edge,
            pltpu.VMEM((2, *far_up.shape), F32),
            pltpu.VMEM((32, width), F32),
            tiles(2 * STEPS + 3, NV),
            tiles(2 * STEPS + 2, 2),
            *state(span + 2 * PAD),
            pltpu.VMEM((2, BLOCK, LANES, LANES), F32),
            pltpu.SemaphoreType.DMA((32,)),
            tiles(FILL),
        ],
        compiler_params=PARAMS,
        cost_estimate=cost(4 * 10**8, 16),
        name="slab",
    )(diag, lower, upper, fields, kappa, before, after, from_up, from_down, far_up, far_down, east, south)


def ring(axis, step):
    size = lax.axis_size(axis)
    return [(i, (i + step) % size) for i in range(size)]


def local(forcing, kappa, diag, lower, upper):
    up, down = pick(lower, upper, forcing)
    before = lax.ppermute(up, "tm", ring("tm", 1))
    after = lax.ppermute(down, "tm", ring("tm", -1))
    pack_up, pack_down = packs(forcing, kappa, down)
    from_down = lax.ppermute(pack_up, "space", ring("space", -1))
    from_up = lax.ppermute(pack_down, "space", ring("space", 1))
    east, south = faces(kappa)
    first, last = corners(before, after, east)
    far_down = lax.ppermute(first, "space", ring("space", -1))
    far_up = lax.ppermute(last, "space", ring("space", 1))
    return slab(diag, lower, upper, forcing, kappa, before, after, from_up, from_down, far_up, far_down, east, south)


def solution(mesh):
    return jax.shard_map(
        local,
        mesh=mesh,
        in_specs=(P("space", "tm", None), P("space", None), P("tm"), P("tm"), P("tm")),
        out_specs=P("space", "tm", None),
        check_vma=False,
    )
```
